256 devices in a mesh: section: 16 (over y, x), expert: 16 (over z, core).
Axes of the slice: x: 4, y: 4, z: 8, core: 2. Of those that a mesh axis runs over, the one named last changes fastest.
Arguments:
- layer_inputs: bfloat16 [16, 16, 128, 4096], P('section', None, 'expert'), may hold values from -6 to 6
- expert_ids: int32 [16, 16, 128, 2], P('section', None, 'expert'), may hold values from 0 to 7, all different within a row; in each aligned block of 8 rows (0 to 7, 8 to 15, ..., all dimensions but the last counted through in order) at most 3 rows name the same one
- gates: bfloat16 [16, 16, 128, 2], P('section', None, 'expert'), may hold values from 0.099609375 to 0.59765625
- w_gate: bfloat16 [16, 4096, 4096], P('section', None, 'expert'), may hold values from -0.09375 to 0.09375
- w_up: bfloat16 [16, 4096, 4096], P('section', None, 'expert'), may hold values from -0.09375 to 0.09375
- w_down: bfloat16 [16, 4096, 4096], P('section', 'expert'), may hold values from -0.25 to 0.25
- out_grad: bfloat16 [16, 128, 4096], P(None, 'expert'), may hold values from -6 to 6
Outputs:
- section_grads: bfloat16 [16, 16, 128, 4096], P('section', None, 'expert')
The draws below stay inside these ranges and needn't reach their ends.
Inputs may be any that keep to these rules, and one draw needn't show every extreme that they name: `expert_ids`: within one micro-batch of one section, the 8 tokens of one expert index name each expert at most 3 times, and in some such groups one expert exactly 3 times; a token's 2 experts differ.
All inputs are finite; a program needn't handle non-finite values.
Results may differ from the reference program's by a relative error of at most 0.035.
Values may be sent and summed in bfloat16 or wider, within the bound.
A program may use at most 64 MiB of HBM per device.

```python
import math
import jax
import jax.numpy as jnp
import numpy as np
from jax import lax

D = 4096
EXPERTS = 8
TOP = 2
FF_WIN = 512
TOK = 8
MB = 16
CAP = 3
SHARDS = 2
SECTION_TOKENS = 128
N_SECTION = 16
N_EXPERT = 16


def shard_levels(own_key, dims, shards, low, largest):
    def one(dim, parts):
        steps = jax.random.uniform(jax.random.fold_in(jax.random.fold_in(own_key, 6), dim), (parts,), jnp.float32, low / len(shards), largest / len(shards))
        return jnp.repeat(jnp.exp(steps), dims[dim] // parts).reshape((-1,) + (1,) * (len(dims) - dim - 1))

    loudness = one(*shards[0])
    for cut in shards[1:]:
        loudness = loudness * one(*cut)
    return loudness


def shared_out(stream_key, own, number, rows, number_of, top, bound, lean):
    order = jax.random.permutation(stream_key, number_of)
    crowded, common = load_shares(number_of, rows * top, bound, lean, True), load_shares(number_of, rows * top, bound, lean, False)
    places = jnp.arange(number_of)

    def named(tallies, turn):
        used = int((tallies > 0).sum())
        fixed = max(1, used // 4)
        shifted = fixed + (places - fixed + turn * (used - fixed)) % max(1, number_of - fixed)
        return jnp.zeros((number_of,), jnp.int32).at[order[jnp.where(places < fixed, places, shifted)]].set(jnp.asarray(tallies, jnp.int32))

    tallies = jnp.where(number % 4 == 0, named(crowded, number // 4), named(common, number - number // 4 - 1))
    mixed = jax.random.permutation(jax.random.fold_in(own, 3), number_of)
    donor, taker = mixed[0:number_of // 2 * 2:2], mixed[1:number_of // 2 * 2:2]
    room = jnp.minimum(tallies[donor] - 1, bound - tallies[taker]) // 2
    room = jnp.where((donor == order[0]) | (taker == order[0]) | (tallies[taker] == 0), 0, jnp.maximum(room, 0))
    shifted = jax.random.randint(jax.random.fold_in(own, 4), (number_of // 2,), 0, 1 << 20) % (room + 1)
    tallies = tallies.at[donor].add(-shifted).at[taker].add(shifted)
    labels = jnp.searchsorted(jnp.cumsum(tallies), jnp.arange(rows * top), side="right").astype(jnp.int32)
    table = labels.reshape(top, rows).T
    table = table[jax.random.permutation(jax.random.fold_in(own, 1), rows)]
    turn = jax.random.randint(jax.random.fold_in(own, 2), (rows, 1), 0, top)
    return jnp.take_along_axis(table, (jnp.arange(top)[None, :] + turn) % top, axis=1)


def load_shares(number_of, total, reach, lean, full):
    loads = [(1 << 20) // math.isqrt(grade ** lean) + 1 for grade in range(1, number_of + 1)]
    largest = reach if full else min(reach, max(-(-total // number_of), total * loads[0] // sum(loads)))
    least = 1 if total - largest >= number_of - 1 else 0
    holding, spare = [largest] + [least] * (number_of - 1), total - largest - least * (number_of - 1)
    while spare > 0:
        candidates = [i for i in range(1, number_of) if holding[i] < largest] or [i for i in range(1, number_of) if holding[i] < reach]
        pool, budget = sum([loads[i] for i in candidates]), spare
        for i in candidates:
            extra = min(reach - holding[i], max(1, budget * loads[i] // pool), spare)
            holding[i] = holding[i] + extra
            spare = spare - extra
    return np.array(holding)


def normal_values(own_key, shape, spread, reach, shards=(), held_as=jnp.bfloat16):
    gain = shard_levels(own_key, shape, shards, -0.22, 0.18) if shards else 1.0
    result = jax.random.normal(own_key, shape, jnp.float32) * spread * gain
    return jnp.minimum(jnp.maximum(result, -reach), reach).astype(held_as)


def setup_inputs(seed: int = 0) -> dict:
    splits = jax.random.split(jax.random.key(seed), 8)
    layer_inputs = normal_values(splits[0], (N_SECTION, MB, SECTION_TOKENS, D), 1.0, 6.0, ((0, 16), (2, 16)))
    expert_ids_keys = jax.random.split(jax.random.fold_in(splits[1], 1), N_SECTION * MB * SECTION_TOKENS // TOK)
    expert_ids_turns = jax.random.permutation(jax.random.fold_in(splits[1], 3), N_SECTION * MB * SECTION_TOKENS // TOK)
    expert_ids = jax.vmap(lambda own, number: shared_out(jax.random.fold_in(splits[1], 2), own, number, TOK, EXPERTS, TOP, CAP, 2))(expert_ids_keys, expert_ids_turns).reshape((N_SECTION, MB, SECTION_TOKENS, TOP))
    gates = jnp.clip(0.099609375 + 0.49804688 * jax.random.uniform(splits[2], (N_SECTION, MB, SECTION_TOKENS, TOP), jnp.float32) ** shard_levels(splits[2], (N_SECTION, MB, SECTION_TOKENS, TOP), ((0, 16), (2, 16)), -0.2, 0.2), 0.099609375, 0.59765625).astype(jnp.bfloat16)
    w_gate = normal_values(splits[3], (N_SECTION, D, EXPERTS * FF_WIN), D ** -0.5, 0.09375, ((0, 16), (2, 16)))
    w_up = normal_values(splits[4], (N_SECTION, D, EXPERTS * FF_WIN), D ** -0.5, 0.09375, ((0, 16), (2, 16)))
    w_down = normal_values(splits[5], (N_SECTION, EXPERTS * FF_WIN, D), FF_WIN ** -0.5, 0.25, ((0, 16), (1, 16)))
    out_grad = normal_values(splits[6], (MB, SECTION_TOKENS, D), 1.0, 6.0, ((1, 16),))
    return dict(layer_inputs=layer_inputs, expert_ids=expert_ids, gates=gates, w_gate=w_gate, w_up=w_up, w_down=w_down, out_grad=out_grad)


def selection(choices):
    experts = jnp.arange(EXPERTS, dtype=jnp.int32)
    onehot = (choices[..., None] == experts).astype(jnp.int32)
    leading = onehot.shape[:-3]
    flattened = onehot.reshape(leading + (TOK * TOP, EXPERTS))
    before = jnp.cumsum(flattened, axis=-2) - flattened
    slot_index = jnp.sum((before * flattened).reshape(onehot.shape), axis=-1)
    places = jnp.arange(CAP, dtype=jnp.int32)
    in_slot = (slot_index[..., None] == places).astype(jnp.int32)
    return onehot[..., None] * in_slot[..., None, :]


def reference(layer_inputs, expert_ids, gates, w_gate, w_up, w_down, out_grad):
    sources = N_EXPERT
    block_units = FF_WIN // SHARDS

    def one_section(incoming, section_data):
        inputs, choices, gate_values, gate_proj, up_proj, down_proj = section_data
        inputs = inputs.reshape(MB, sources, TOK, D).astype(jnp.float32)
        selected = selection(choices.reshape(MB, sources, TOK, TOP)).astype(jnp.float32)
        dispatch = jnp.sum(selected, axis=3)
        weights = gate_values.reshape(MB, sources, TOK, TOP).astype(jnp.float32)
        combine = jnp.sum(selected * weights[..., None, None], axis=3)
        gate_proj = gate_proj.astype(jnp.float32).reshape(D, EXPERTS, FF_WIN)
        up_proj = up_proj.astype(jnp.float32).reshape(D, EXPERTS, FF_WIN)
        down_proj = down_proj.astype(jnp.float32).reshape(EXPERTS, FF_WIN, D)
        token_rows = jnp.einsum('mstec,mstd->emscd', dispatch, inputs).reshape(EXPERTS, -1, D)
        pre_gate = jnp.einsum('erd,def->erf', token_rows, gate_proj)
        pre_up = jnp.einsum('erd,def->erf', token_rows, up_proj)
        sigmoid_gate = jax.nn.sigmoid(pre_gate)
        act = pre_gate * sigmoid_gate
        coef = pre_up * (sigmoid_gate * (1.0 + pre_gate * (1.0 - sigmoid_gate)))
        grad_out = incoming.astype(jnp.float32).reshape(MB, sources, TOK, D)
        grad_rows = jnp.einsum('mstec,mstd->emscd', dispatch, grad_out).reshape(EXPERTS, -1, D)
        down_grad = jnp.einsum('erd,efd->erf', grad_rows, down_proj)
        dgate = lax.optimization_barrier((down_grad * coef).astype(jnp.bfloat16)).astype(jnp.float32)
        dup = lax.optimization_barrier((down_grad * act).astype(jnp.bfloat16)).astype(jnp.float32)
        dgate = dgate.reshape(EXPERTS, -1, SHARDS, block_units)
        dup = dup.reshape(EXPERTS, -1, SHARDS, block_units)
        gate_blocks = gate_proj.reshape(D, EXPERTS, SHARDS, block_units)
        up_blocks = up_proj.reshape(D, EXPERTS, SHARDS, block_units)
        back = jnp.einsum('erkh,dekh->erkd', dgate, gate_blocks) + jnp.einsum('erkh,dekh->erkd', dup, up_blocks)
        back = lax.optimization_barrier(back.astype(jnp.bfloat16)).astype(jnp.float32)
        back = back.reshape(EXPERTS, MB, sources, CAP, SHARDS, D)
        mixed = jnp.einsum('mstec,emsckd->mstd', combine, back)
        grad_in = (grad_out + mixed).astype(jnp.bfloat16).reshape(MB, sources * TOK, D)
        return grad_in, grad_in

    section_data = (layer_inputs, expert_ids, gates, w_gate, w_up, w_down)
    final_grad, section_grads = lax.scan(one_section, out_grad, section_data, reverse=True)
    return section_grads
```

```python
import jax
import jax.numpy as jnp
from jax import lax
from jax.experimental import pallas as pl
from jax.experimental.pallas import tpu as pltpu
from jax.sharding import PartitionSpec as P

EXPERTS = 8
CAP = 3
SLOTS = EXPERTS * CAP
MB = 16
TOK = 8
D = 4096
FOLD = 16
LANES = 128
HALF = FOLD * LANES
ROWS = CAP * FOLD
PAIR_ROWS = SLOTS * FOLD
TOK_ROWS = TOK * FOLD
PAD = 32
HID = 256
LAST = 15
FAR_FIRST = (4, 3, 5, 2, 6, 1, 7)
MESH = pl.DeviceIdType.MESH
BF16 = jnp.bfloat16
F32 = jnp.float32


def matmul(a, b):
    return lax.dot_general(a, b, (((1,), (0,)), ((), ())), preferred_element_type=F32)


def iota(shape, dim):
    return lax.broadcasted_iota(jnp.int32, shape, dim)


def chain_kernel(
    x_ref, og_ref, disp_ref, comb_ref, wg_hbm, wu_hbm, wd_hbm, wgt_hbm, wut_hbm,
    out_ref,
    wg, wu, wd, wgt, wut, comb_next,
    send_x, send_g, send_r, recv_x, recv_g, recv_r, recv_last,
    g_prev, g_here, saved, lhs, folded, unfold_mat, fold_mat,
    own_sems, swap_send, swap_recv, comb_send, comb_recv,
    x_send, g_send, r_send, p_send, o_send,
    x_recv, g_recv, r_recv, last_recv, p_recv, o_recv,
):
    s = lax.axis_index("section")
    i = lax.axis_index("expert")
    z = i // 2
    c = lax.rem(i, 2)
    up = lax.rem(s + 1, LAST + 1)
    down = lax.rem(s + LAST, LAST + 1)

    def at(section, chip):
        return {"section": section, "expert": chip * 2 + c}

    sibling = {"section": s, "expert": z * 2 + 1 - c}

    barrier = pltpu.get_barrier_semaphore()
    pl.semaphore_signal(barrier, inc=1, device_id=sibling, device_id_type=MESH)
    for d in range(1, EXPERTS):
        pl.semaphore_signal(barrier, inc=1, device_id=at(s, lax.rem(z + d, EXPERTS)), device_id_type=MESH)
    for d in range(EXPERTS):
        pl.semaphore_signal(barrier, inc=1, device_id=at(up, lax.rem(z + d, EXPERTS)), device_id_type=MESH)
        pl.semaphore_signal(barrier, inc=1, device_id=at(down, lax.rem(z + d, EXPERTS)), device_id_type=MESH)
    pl.semaphore_wait(barrier, 1 + 3 * EXPERTS - 1)

    weights = ((wg_hbm, wg), (wu_hbm, wu), (wd_hbm, wd), (wgt_hbm, wgt), (wut_hbm, wut))

    def own_copy(n):
        return pltpu.make_async_copy(weights[n][0], weights[n][1].at[c], own_sems.at[n])

    def swap_copy(n):
        return pltpu.make_async_remote_copy(
            src_ref=weights[n][0], dst_ref=weights[n][1].at[c], send_sem=swap_send.at[n],
            recv_sem=swap_recv.at[n], device_id=sibling, device_id_type=MESH,
        )

    def weights_ready(n):
        own_copy(n).wait()
        swap_copy(n).wait_recv()

    for n in range(5):
        swap_copy(n).start()
        own_copy(n).start()

    def comb_copy():
        return pltpu.make_async_remote_copy(
            src_ref=comb_ref, dst_ref=comb_next, send_sem=comb_send, recv_sem=comb_recv,
            device_id=at(down, z), device_id_type=MESH,
        )

    @pl.when(s > 0)
    def _():
        comb_copy().start()

    r0, r1 = iota((FOLD * PAD, PAIR_ROWS), 0), iota((FOLD * PAD, PAIR_ROWS), 1)
    hit = ((r0 & 31) == (r1 >> 4)) & ((r0 >> 5) == (r1 & 15))
    unfold_mat[...] = jnp.where(hit, 1.0, 0.0).astype(BF16)
    r0, r1 = iota((PAIR_ROWS, FOLD * PAD), 0), iota((PAIR_ROWS, FOLD * PAD), 1)
    hit = ((r1 & 31) == (r0 >> 4)) & ((r1 >> 5) == (r0 & 15))
    fold_mat[...] = jnp.where(hit, 1.0, 0.0).astype(BF16)

    def dispatch_matrix(m):
        rows = iota((PAIR_ROWS, PAD), 0) >> 4
        spread = jnp.where(rows == iota((PAIR_ROWS, PAD), 1), 1.0, 0.0).astype(BF16)
        wide = matmul(spread, disp_ref[m])
        same = (iota((PAIR_ROWS, TOK_ROWS), 0) & 15) == (iota((PAIR_ROWS, TOK_ROWS), 1) & 15)
        return jnp.where(same, wide, 0.0).astype(BF16)

    def combine_matrix(ref, m):
        columns = iota((LANES, PAIR_ROWS), 1) >> 4
        spread = jnp.where(columns == iota((LANES, PAIR_ROWS), 0), 1.0, 0.0).astype(BF16)
        wide = matmul(ref[m], spread)
        same = (iota((TOK_ROWS, PAIR_ROWS), 0) & 15) == (iota((TOK_ROWS, PAIR_ROWS), 1) & 15)
        return jnp.where(same, wide, 0.0).astype(BF16)

    def half(h):
        return pl.ds(h * ROWS, ROWS)

    def part(value):
        return value.astype(BF16).reshape(EXPERTS, ROWS, LANES)

    def spread_x(m):
        matrix = dispatch_matrix(m)
        for h in range(2):
            send_x[m, :, half(h), :] = part(matmul(matrix, x_ref[m, h]))
        for d in FAR_FIRST:
            to = lax.rem(z + d, EXPERTS)
            pltpu.make_async_remote_copy(
                src_ref=send_x.at[m, to], dst_ref=recv_x.at[m, z], send_sem=x_send,
                recv_sem=x_recv.at[m], device_id=at(s, to), device_id_type=MESH,
            ).start()
        pltpu.make_async_copy(send_x.at[m, z], recv_x.at[m, z], x_recv.at[m]).start()

    def spread_g(m, h, matrix, rows):
        send_g[m, :, half(h), :] = part(matmul(matrix, rows))
        for d in FAR_FIRST:
            to = lax.rem(z + d, EXPERTS)
            pltpu.make_async_remote_copy(
                src_ref=send_g.at[m, to, half(h)], dst_ref=recv_g.at[m, z, half(h)], send_sem=g_send,
                recv_sem=g_recv.at[m, h], device_id=at(s, to), device_id_type=MESH,
            ).start()
        pltpu.make_async_copy(
            send_g.at[m, z, half(h)], recv_g.at[m, z, half(h)], g_recv.at[m, h]
        ).start()

    def arrived(ref, m, h, sem):
        whole = ref.at[m, :, half(h)]
        pltpu.make_async_copy(whole, whole, sem.at[m, h]).wait()

    def unfold(ref, m, h):
        rows = matmul(unfold_mat[...], ref[m, :, half(h), :].reshape(PAIR_ROWS, LANES)).astype(BF16)
        for j in range(FOLD):
            lhs[:, h * HALF + j * LANES : h * HALF + (j + 1) * LANES] = rows[j * PAD : (j + 1) * PAD]

    def forward(m):
        pltpu.make_async_copy(recv_x.at[m], recv_x.at[m], x_recv.at[m]).wait()
        for h in range(2):
            unfold(recv_x, m, h)
        for k in range(2):
            gate = matmul(lhs[...], wg[k])
            value = matmul(lhs[...], wu[k])
            sig = jax.nn.sigmoid(gate)
            saved[m, 0, :, k * HID : (k + 1) * HID] = gate * sig
            saved[m, 1, :, k * HID : (k + 1) * HID] = value * (sig * (1.0 + gate * (1.0 - sig)))

    def send_back(m, h):
        @pl.when(s > 0)
        def _():
            for d in FAR_FIRST + (0,):
                to = lax.rem(z + d, EXPERTS)
                pltpu.make_async_remote_copy(
                    src_ref=send_r.at[m, to, half(h)], dst_ref=recv_r.at[m, z, half(h)], send_sem=r_send,
                    recv_sem=r_recv.at[m, h], device_id=at(down, to), device_id_type=MESH,
                ).start()

        @pl.when(s == 0)
        def _():
            for d in FAR_FIRST:
                to = lax.rem(z + d, EXPERTS)
                pltpu.make_async_remote_copy(
                    src_ref=send_r.at[m, to, half(h)], dst_ref=recv_last.at[m, z, half(h)], send_sem=r_send,
                    recv_sem=last_recv.at[m, h], device_id=at(s, to), device_id_type=MESH,
                ).start()
            pltpu.make_async_copy(
                send_r.at[m, z, half(h)], recv_last.at[m, z, half(h)], last_recv.at[m, h]
            ).start()

    def backward(m):
        sums = [None, None]
        for h in range(2):
            arrived(recv_g, m, h, g_recv)
            unfold(recv_g, m, h)
            columns = slice(h * HALF, (h + 1) * HALF)
            for k in range(2):
                term = matmul(lhs[:, columns], wd[k, columns, :])
                sums[k] = term if h == 0 else sums[k] + term
        pieces = []
        for k in range(2):
            hidden = slice(k * HID, (k + 1) * HID)
            pieces.append(
                ((sums[k] * saved[m, 1, :, hidden]).astype(BF16), (sums[k] * saved[m, 0, :, hidden]).astype(BF16))
            )
        width = 4 * LANES
        for h in range(2):
            for n in range(HALF // width):
                columns = slice(h * HALF + n * width, h * HALF + (n + 1) * width)
                total = matmul(pieces[0][0], wgt[0, :, columns])
                total += matmul(pieces[0][1], wut[0, :, columns])
                total += matmul(pieces[1][0], wgt[1, :, columns])
                total += matmul(pieces[1][1], wut[1, :, columns])
                rows = total.astype(BF16)
                for q in range(4):
                    j = n * 4 + q
                    folded[j * PAD : (j + 1) * PAD, :] = rows[:, q * LANES : (q + 1) * LANES]
            send_r[m, :, half(h), :] = part(matmul(fold_mat[...], folded[...]))
            send_back(m, h)

    def pass_on(m, h):
        pltpu.make_async_remote_copy(
            src_ref=g_here.at[m, h], dst_ref=out_ref.at[m, h], send_sem=o_send, recv_sem=o_recv,
            device_id=at(up, z), device_id_type=MESH,
        ).start()

        @pl.when(s > 0)
        def _():
            pltpu.make_async_remote_copy(
                src_ref=g_here.at[m, h], dst_ref=g_prev.at[m, h], send_sem=p_send,
                recv_sem=p_recv.at[m, h], device_id=at(down, z), device_id_type=MESH,
            ).start()

    def gather(m):
        dispatch = dispatch_matrix(m)
        combine = combine_matrix(comb_next, m)
        for h in range(2):
            @pl.when(s < LAST - 1)
            def _():
                pltpu.make_async_copy(g_prev.at[m, h], g_prev.at[m, h], p_recv.at[m, h]).wait()

            arrived(recv_r, m, h, r_recv)
            mixed = matmul(combine, recv_r[m, :, half(h), :].reshape(PAIR_ROWS, LANES))
            rows = (g_prev[m, h].astype(F32) + mixed).astype(BF16)
            g_here[m, h] = rows
            spread_g(m, h, dispatch, rows)
        for h in range(2):
            pass_on(m, h)

    def first_gather(m):
        matrix = dispatch_matrix(m)
        for h in range(2):
            spread_g(m, h, matrix, og_ref[m, h])

    def finish(m):
        combine = combine_matrix(comb_ref, m)
        for h in range(2):
            arrived(recv_last, m, h, last_recv)
            mixed = matmul(combine, recv_last[m, :, half(h), :].reshape(PAIR_ROWS, LANES))
            out_ref[m, h] = (g_here[m, h].astype(F32) + mixed).astype(BF16)

    ahead = jnp.minimum(MB, 1 + 4 * (LAST - s))
    x_ahead = jnp.minimum(MB, ahead + 1)

    spread_x(0)

    @pl.when(s == LAST)
    def _():
        first_gather(0)

    def more_x(m, carry):
        spread_x(m)
        return carry

    lax.fori_loop(1, x_ahead, more_x, 0)

    @pl.when(s == LAST - 1)
    def _():
        g_prev[...] = og_ref[...]

    weights_ready(0)
    weights_ready(1)

    def more_forward(m, carry):
        forward(m)
        return carry

    lax.fori_loop(0, ahead, more_forward, 0)
    weights_ready(2)
    weights_ready(3)
    weights_ready(4)

    @pl.when(s < LAST)
    def _():
        comb_copy().wait_recv()

    def step(m, carry):
        @pl.when(s < LAST)
        def _():
            gather(m)

        @pl.when((s == LAST) & (m + 1 < MB))
        def _():
            first_gather(m + 1)

        @pl.when(m + x_ahead < MB)
        def _():
            spread_x(m + x_ahead)

        backward(m)

        @pl.when(m + ahead < MB)
        def _():
            forward(m + ahead)

        @pl.when((s == 0) & (m > 0))
        def _():
            finish(m - 1)

        return carry

    lax.fori_loop(0, MB, step, 0)

    @pl.when(s == 0)
    def _():
        finish(MB - 1)

    for n in range(5):
        swap_copy(n).wait_send()

    def drain(ref, sem):
        pltpu.make_async_copy(ref, ref, sem).wait()

    drain(send_x.at[:, pl.ds(0, EXPERTS - 1)], x_send)
    drain(send_g.at[:, pl.ds(0, EXPERTS - 1)], g_send)

    @pl.when(s > 0)
    def _():
        comb_copy().wait_send()
        drain(send_r, r_send)
        drain(out_ref, o_recv)

    @pl.when(s == 0)
    def _():
        drain(send_r.at[:, pl.ds(0, EXPERTS - 1)], r_send)

    @pl.when(s < LAST)
    def _():
        drain(g_here, o_send)

    @pl.when((s > 0) & (s < LAST))
    def _():
        drain(g_here, p_send)


def chain(x, og, disp, comb, wg, wu, wd, wgt, wut):
    vmem = pl.BlockSpec(memory_space=pltpu.VMEM)
    anywhere = pl.BlockSpec(memory_space=pl.ANY)
    blocks = (MB, EXPERTS, 2 * ROWS, LANES)
    rows = (MB, 2, TOK_ROWS, LANES)
    dma = pltpu.SemaphoreType.DMA
    return pl.pallas_call(
        chain_kernel,
        out_shape=jax.ShapeDtypeStruct(rows, BF16),
        in_specs=[vmem] * 4 + [anywhere] * 5,
        out_specs=vmem,
        scratch_shapes=[
            pltpu.VMEM((2, D, HID), BF16),
            pltpu.VMEM((2, D, HID), BF16),
            pltpu.VMEM((2, D, HID), BF16),
            pltpu.VMEM((2, HID, D), BF16),
            pltpu.VMEM((2, HID, D), BF16),
            pltpu.VMEM((MB, TOK_ROWS, LANES), BF16),
        ]
        + [pltpu.VMEM(blocks, BF16)] * 7
        + [
            pltpu.VMEM(rows, BF16),
            pltpu.VMEM(rows, BF16),
            pltpu.VMEM((MB, 2, PAD, 2 * HID), F32),
            pltpu.VMEM((PAD, D), BF16),
            pltpu.VMEM((FOLD * PAD, LANES), BF16),
            pltpu.VMEM((FOLD * PAD, PAIR_ROWS), BF16),
            pltpu.VMEM((PAIR_ROWS, FOLD * PAD), BF16),
            dma((5,)),
            dma((5,)),
            dma((5,)),
            dma,
            dma,
            dma,
            dma,
            dma,
            dma,
            dma,
            dma((MB,)),
            dma((MB, 2)),
            dma((MB, 2)),
            dma((MB, 2)),
            dma((MB, 2)),
            dma,
        ],
        compiler_params=pltpu.CompilerParams(
            collective_id=0, has_side_effects=True, vmem_limit_bytes=60 * 1024 * 1024
        ),
    )(x, og, disp, comb, wg, wu, wd, wgt, wut)


def fold_rows(x):
    return x.reshape(MB, TOK, 2, FOLD, LANES).transpose(0, 2, 1, 3, 4).reshape(MB, 2, TOK_ROWS, LANES)


def on_device(layer_inputs, expert_ids, gates, w_gate, w_up, w_down, out_grad):
    pairs = expert_ids[0].reshape(MB, TOK * 2)
    token = jnp.arange(TOK * 2, dtype=jnp.int32) // 2
    same = (pairs[:, :, None] == pairs[:, None, :]) & (token[None, :] < token[:, None])[None]
    slot = jnp.sum(same.astype(jnp.int32), axis=-1)
    target = jnp.repeat((pairs * CAP + slot).reshape(MB, TOK, 2), FOLD, axis=1)
    gate = jnp.repeat(gates[0], FOLD, axis=1)
    down = jnp.arange(PAD, dtype=jnp.int32)[None, :, None]
    across = jnp.arange(LANES, dtype=jnp.int32)[None, None, :]
    disp = ((target[:, None, :, 0] == down) | (target[:, None, :, 1] == down)).astype(BF16)
    zero = jnp.zeros((), BF16)
    comb = jnp.where(
        target[:, :, 0:1] == across, gate[:, :, 0:1],
        jnp.where(target[:, :, 1:2] == across, gate[:, :, 1:2], zero),
    )
    out = chain(
        fold_rows(layer_inputs[0]), fold_rows(out_grad), disp, comb,
        w_gate[0], w_up[0], w_down[0].T, w_gate[0].T, w_up[0].T,
    )
    out = out.reshape(MB, 2, TOK, FOLD, LANES).transpose(0, 2, 1, 3, 4).reshape(MB, TOK, D)
    return out[None]


def solution(mesh):
    placed = (
        P("section", None, "expert", None),
        P("section", None, "expert", None),
        P("section", None, "expert", None),
        P("section", None, "expert"),
        P("section", None, "expert"),
        P("section", "expert", None),
        P(None, "expert", None),
    )
    return jax.shard_map(
        on_device,
        mesh=mesh,
        in_specs=placed,
        out_specs=P("section", None, "expert", None),
        check_vma=False,
    )
```

```python
import jax
import jax.numpy as jnp
from jax import lax
from jax.experimental import pallas as pl
from jax.experimental.pallas import tpu as pltpu
from jax.sharding import PartitionSpec as P

EXPERTS = 8
CAP = 3
SLOTS = EXPERTS * CAP
MB = 16
PAIRS = MB // 2
TOK = 8
D = 4096
FOLD = 16
LANES = 128
HALF = FOLD * LANES
ROWS = CAP * FOLD
PAIR_ROWS = SLOTS * FOLD
TOK_ROWS = TOK * FOLD
PAD = 32
HID = 256
LINES = 16
LAST = LINES - 1
FIRST = 3
FAR_FIRST = (4, 3, 5, 2, 6, 1, 7)
MESH = pl.DeviceIdType.MESH
BF16 = jnp.bfloat16
F32 = jnp.float32


def matmul(a, b):
    return lax.dot_general(a, b, (((1,), (0,)), ((), ())), preferred_element_type=F32)


def iota(shape, dim):
    return lax.broadcasted_iota(jnp.int32, shape, dim)


def chain_kernel(
    x_ref, og_ref, pairs_ref, wg_hbm, wu_hbm, wd_hbm,
    out_ref,
    wg, wu, wd, wgt, wut, wd_raw, info, comb_info, top_info, x_help,
    send_x, send_g, send_r, recv_x, recv_g, recv_r, recv_last,
    g_prev, g_here, saved, lhs, folded, unfold_mat, fold_mat,
    own_sems, swap_send, swap_recv, info_send, info_recv, help_send, help_recv,
    x_send, g_send, r_send, p_send, o_send,
    x_recv, g_recv, r_recv, last_recv, p_recv, o_recv, turn,
):
    line = lax.axis_index("section")
    i = lax.axis_index("expert")
    z = i // 2
    c = lax.rem(i, 2)

    def off(by):
        return lax.rem(line + by, LINES)

    def at(section, chip):
        return {"section": section, "expert": chip * 2 + c}

    def other(d):
        return lax.rem(z + d, EXPERTS)

    first = line == FIRST
    top = line == LAST
    helped = (line >= 12) & (line < LAST)
    helper = line < 3
    sibling = {"section": line, "expert": z * 2 + 1 - c}
    barrier = pltpu.get_barrier_semaphore()

    def greet(device):
        pl.semaphore_signal(barrier, inc=1, device_id=device, device_id_type=MESH)

    greet(sibling)
    for d in range(1, EXPERTS):
        greet(at(line, other(d)))
    for d in range(EXPERTS):
        greet(at(off(1), other(d)))
        greet(at(off(15), other(d)))

    @pl.when(top)
    def _():
        for d in range(EXPERTS):
            greet(at(FIRST, other(d)))

    @pl.when(first)
    def _():
        for d in range(EXPERTS):
            greet(at(LAST, other(d)))

    @pl.when(helped)
    def _():
        for d in range(EXPERTS):
            greet(at(off(4), other(d)))

    @pl.when(helper)
    def _():
        greet(at(off(12), z))

    raw = ((wg_hbm, wg.at[c]), (wu_hbm, wu.at[c]), (wd_hbm, wd_raw))

    def own_copy(n):
        return pltpu.make_async_copy(raw[n][0], raw[n][1], own_sems.at[n])

    for n in (2, 0, 1):
        own_copy(n).start()

    whole = (wg, wu, wd, wgt, wut)

    def swap_copy(n):
        return pltpu.make_async_remote_copy(
            src_ref=whole[n].at[c], dst_ref=whole[n].at[c], send_sem=swap_send.at[n],
            recv_sem=swap_recv.at[n], device_id=sibling, device_id_type=MESH,
        )

    ids = (pairs_ref[0], pairs_ref[1])
    token = iota((MB, LANES), 1) & 7
    slots = [jnp.zeros((MB, LANES), F32), jnp.zeros((MB, LANES), F32)]
    for r in range(1, TOK):
        for k in range(2):
            earlier = pltpu.roll(ids[k], r, 1)
            for q in range(2):
                slots[q] += jnp.where((earlier == ids[q]) & (token >= r), 1.0, 0.0)
    for q in range(2):
        info[q] = ids[q] * CAP + slots[q]
        info[2 + q] = pairs_ref[2 + q]

    r0, r1 = iota((FOLD * PAD, PAIR_ROWS), 0), iota((FOLD * PAD, PAIR_ROWS), 1)
    hit = ((r0 & 31) == (r1 >> 4)) & ((r0 >> 5) == (r1 & 15))
    unfold_mat[...] = jnp.where(hit, 1.0, 0.0).astype(BF16)
    r0, r1 = iota((PAIR_ROWS, FOLD * PAD), 0), iota((PAIR_ROWS, FOLD * PAD), 1)
    hit = ((r1 & 31) == (r0 >> 4)) & ((r1 >> 5) == (r0 & 15))
    fold_mat[...] = jnp.where(hit, 1.0, 0.0).astype(BF16)

    extra = jnp.where(top | first | helper, EXPERTS, jnp.where(helped, 1, 0))
    pl.semaphore_wait(barrier, 3 * EXPERTS + extra)

    def info_copy(n):
        return pltpu.make_async_remote_copy(
            src_ref=info, dst_ref=(comb_info, top_info, top_info)[n], send_sem=info_send.at[n],
            recv_sem=info_recv.at[n], device_id=at((off(15), FIRST, off(4))[n], z), device_id_type=MESH,
        )

    @pl.when(line > 0)
    def _():
        info_copy(0).start()

    @pl.when(top)
    def _():
        info_copy(1).start()

    @pl.when(helped)
    def _():
        info_copy(2).start()

    def matrix(ref, m, first, second):
        place = (iota((PAIR_ROWS, TOK_ROWS), 0) >> 4).astype(F32)
        same = (iota((PAIR_ROWS, TOK_ROWS), 0) & 15) == (iota((PAIR_ROWS, TOK_ROWS), 1) >> 3)
        row = pl.ds(m, 1)
        value = jnp.where(ref[0, row] == place, first, jnp.where(ref[1, row] == place, second, 0.0))
        return jnp.where(same, value, 0.0)

    def dispatch_matrix(ref, m):
        return matrix(ref, m, 1.0, 1.0).astype(BF16)

    def combine_matrix(ref, m):
        row = pl.ds(m, 1)
        return matrix(ref, m, ref[2, row], ref[3, row]).T.astype(BF16)

    def half(h):
        return pl.ds(h * ROWS, ROWS)

    def part(value):
        return value.astype(BF16).reshape(EXPERTS, ROWS, LANES)

    def fold_pair(ref, p):
        both = ref[pl.ds(pl.multiple_of(p * 2 * TOK, 2 * TOK), 2 * TOK), :].astype(F32)
        result = []
        for b in range(2):
            rows = both[b * TOK : (b + 1) * TOK]
            halves = []
            for h in range(2):
                columns = [rows[:, h * HALF + j * LANES : h * HALF + (j + 1) * LANES] for j in range(FOLD)]
                halves.append(jnp.concatenate(columns, axis=0).astype(BF16))
            result.append(halves)
        return result

    def fill_x(ref, p, from_info):
        values = fold_pair(ref, p)
        for b in range(2):
            dispatch = dispatch_matrix(from_info, p * 2 + b)
            for h in range(2):
                send_x[p, :, pl.ds((b * 2 + h) * ROWS, ROWS), :] = part(matmul(dispatch, values[b][h]))

    def x_copy(p, to, to_line):
        return pltpu.make_async_remote_copy(
            src_ref=send_x.at[p, to], dst_ref=recv_x.at[p, z], send_sem=x_send,
            recv_sem=x_recv.at[p], device_id=at(to_line, to), device_id_type=MESH,
        )

    def pair_rows(p):
        return pl.ds(pl.multiple_of(p * 2 * TOK, 2 * TOK), 2 * TOK)

    def help_copy(p):
        return pltpu.make_async_remote_copy(
            src_ref=x_ref.at[pair_rows(p)], dst_ref=x_help.at[pair_rows(p)], send_sem=help_send,
            recv_sem=help_recv.at[p], device_id=at(off(4), z), device_id_type=MESH,
        )

    def spread_x(p):
        fill_x(x_ref, p, info)
        for d in FAR_FIRST:
            x_copy(p, other(d), line).start()
        pltpu.make_async_copy(send_x.at[p, z], recv_x.at[p, z], x_recv.at[p]).start()

    def g_copy(m, h, to, to_line):
        return pltpu.make_async_remote_copy(
            src_ref=send_g.at[m, to, half(h)], dst_ref=recv_g.at[m, z, half(h)], send_sem=g_send,
            recv_sem=g_recv.at[m, h], device_id=at(to_line, to), device_id_type=MESH,
        )

    def spread_g(m, h, dispatch, rows):
        send_g[m, :, half(h), :] = part(matmul(dispatch, rows))
        for d in FAR_FIRST:
            g_copy(m, h, other(d), line).start()
        pltpu.make_async_copy(
            send_g.at[m, z, half(h)], recv_g.at[m, z, half(h)], g_recv.at[m, h]
        ).start()

    def spread_top(m, h, dispatch, rows):
        send_g[m, :, half(h), :] = part(matmul(dispatch, rows))
        for d in FAR_FIRST + (0,):
            g_copy(m, h, other(d), LAST).start()

    def arrived(ref, m, h, sem):
        block = ref.at[m, :, half(h)]
        pltpu.make_async_copy(block, block, sem.at[m, h]).wait()

    def drain(ref, sem):
        pltpu.make_async_copy(ref, ref, sem).wait()

    def unfold(rows, b, h):
        rows = matmul(unfold_mat[...], rows.reshape(PAIR_ROWS, LANES)).astype(BF16)
        for j in range(FOLD):
            columns = slice(h * HALF + j * LANES, h * HALF + (j + 1) * LANES)
            lhs[b * PAD : (b + 1) * PAD, columns] = rows[j * PAD : (j + 1) * PAD]

    def forward(p):
        drain(recv_x.at[p], x_recv.at[p])
        for b in range(2):
            for h in range(2):
                unfold(recv_x[p, :, pl.ds((b * 2 + h) * ROWS, ROWS), :], b, h)
        for k in range(2):
            hidden = slice(k * HID, (k + 1) * HID)
            gate = matmul(lhs[...], wg[k])
            value = matmul(lhs[...], wu[k])
            sig = jax.nn.sigmoid(gate)
            act = gate * sig
            coef = value * (sig * (1.0 + gate * (1.0 - sig)))
            for b in range(2):
                saved[p * 2 + b, 0, :, hidden] = act[b * PAD : (b + 1) * PAD]
                saved[p * 2 + b, 1, :, hidden] = coef[b * PAD : (b + 1) * PAD]

    def send_back(m, h):
        @pl.when(line > 0)
        def _():
            for d in FAR_FIRST + (0,):
                to = other(d)
                pltpu.make_async_remote_copy(
                    src_ref=send_r.at[m, to, half(h)], dst_ref=recv_r.at[m, z, half(h)], send_sem=r_send,
                    recv_sem=r_recv.at[m, h], device_id=at(off(15), to), device_id_type=MESH,
                ).start()

        @pl.when(line == 0)
        def _():
            for d in FAR_FIRST:
                to = other(d)
                pltpu.make_async_remote_copy(
                    src_ref=send_r.at[m, to, half(h)], dst_ref=recv_last.at[m, z, half(h)], send_sem=r_send,
                    recv_sem=last_recv.at[m, h], device_id=at(line, to), device_id_type=MESH,
                ).start()
            pltpu.make_async_copy(
                send_r.at[m, z, half(h)], recv_last.at[m, z, half(h)], last_recv.at[m, h]
            ).start()

    def backward(m):
        sums = [None, None]
        for h in range(2):
            arrived(recv_g, m, h, g_recv)
            unfold(recv_g[m, :, half(h), :], 0, h)
            columns = slice(h * HALF, (h + 1) * HALF)
            for k in range(2):
                term = matmul(lhs[:PAD, columns], wd[k, columns, :])
                sums[k] = term if h == 0 else sums[k] + term

        @pl.when((line < LAST) & (c == 0))
        def _():
            pl.semaphore_signal(turn, inc=1, device_id=sibling, device_id_type=MESH)

        pieces = []
        for k in range(2):
            hidden = slice(k * HID, (k + 1) * HID)
            pieces.append(
                ((sums[k] * saved[m, 1, :, hidden]).astype(BF16), (sums[k] * saved[m, 0, :, hidden]).astype(BF16))
            )
        width = 4 * LANES
        for h in range(2):
            for n in range(HALF // width):
                columns = slice(h * HALF + n * width, h * HALF + (n + 1) * width)
                total = matmul(pieces[0][0], wgt[0, :, columns])
                total += matmul(pieces[0][1], wut[0, :, columns])
                total += matmul(pieces[1][0], wgt[1, :, columns])
                total += matmul(pieces[1][1], wut[1, :, columns])
                rows = total.astype(BF16)
                for q in range(4):
                    j = n * 4 + q
                    folded[j * PAD : (j + 1) * PAD, :] = rows[:, q * LANES : (q + 1) * LANES]
            send_r[m, :, half(h), :] = part(matmul(fold_mat[...], folded[...]))
            send_back(m, h)

    def home(m):
        dispatch = dispatch_matrix(info, m)
        combine = combine_matrix(comb_info, m)

        @pl.when(c == 1)
        def _():
            pl.semaphore_wait(turn, 1)

        for h in range(2):
            @pl.when(line < LAST - 1)
            def _():
                drain(g_prev.at[m, h], p_recv.at[m, h])

            arrived(recv_r, m, h, r_recv)
            mixed = matmul(combine, recv_r[m, :, half(h), :].reshape(PAIR_ROWS, LANES))
            rows = (g_prev[m, h].astype(F32) + mixed).astype(BF16)
            g_here[m, h] = rows
            spread_g(m, h, dispatch, rows)

    def pass_on(m):
        @pl.when(line > 0)
        def _():
            for h in range(2):
                pltpu.make_async_remote_copy(
                    src_ref=g_here.at[m, h], dst_ref=g_prev.at[m, h], send_sem=p_send,
                    recv_sem=p_recv.at[m, h], device_id=at(off(15), z), device_id_type=MESH,
                ).start()

        pltpu.make_async_remote_copy(
            src_ref=g_here.at[m], dst_ref=out_ref.at[m], send_sem=o_send, recv_sem=o_recv,
            device_id=at(off(1), z), device_id_type=MESH,
        ).start()

    def finish(m):
        combine = combine_matrix(info, m)
        for h in range(2):
            arrived(recv_last, m, h, last_recv)
            mixed = matmul(combine, recv_last[m, :, half(h), :].reshape(PAIR_ROWS, LANES))
            out_ref[m, h] = (g_here[m, h].astype(F32) + mixed).astype(BF16)

    def loop(low, high, body):
        def run(n, carry):
            body(n)
            return carry

        lax.fori_loop(low, high, run, 0)

    @pl.when(line >= 12)
    def _():
        spread_x(0)

    @pl.when(helped)
    def _():
        loop(1, PAIRS, lambda p: help_copy(p).start())

    own_copy(0).wait()
    swap_copy(0).start()
    own_copy(1).wait()
    swap_copy(1).start()

    @pl.when(first)
    def _():
        info_copy(1).wait_recv()

        def start(p):
            values = fold_pair(og_ref, p)
            for b in range(2):
                dispatch = dispatch_matrix(top_info, p * 2 + b)
                for h in range(2):
                    spread_top(p * 2 + b, h, dispatch, values[b][h])

        loop(0, PAIRS, start)

    own_copy(2).wait()

    def turn_down(n):
        columns = pl.ds(pl.multiple_of(n * HID, HID), HID)
        wd[c, columns, :] = wd_raw[:, columns].T

    loop(0, D // HID, turn_down)
    swap_copy(2).start()

    def turn_up(n):
        rows = pl.ds(pl.multiple_of(n * HID, HID), HID)
        wgt[c, :, rows] = wg[c, rows, :].T
        wut[c, :, rows] = wu[c, rows, :].T

    loop(0, D // HID, turn_up)
    swap_copy(3).start()
    swap_copy(4).start()

    @pl.when(helper)
    def _():
        info_copy(2).wait_recv()

        def start(p):
            drain(x_help.at[pair_rows(p)], help_recv.at[p])
            fill_x(x_help, p, top_info)
            for d in FAR_FIRST + (0,):
                x_copy(p, other(d), off(12)).start()
            drain(send_x.at[p], x_send)

        loop(1, PAIRS, start)

    @pl.when(line == LAST - 1)
    def _():
        def start(p):
            values = fold_pair(og_ref, p)
            for b in range(2):
                for h in range(2):
                    g_prev[p * 2 + b, h] = values[b][h]

        loop(0, PAIRS, start)

    @pl.when(first)
    def _():
        drain(send_g, g_send)

    ahead = jnp.where(helped, 1 + LAST - line, jnp.minimum(PAIRS, 1 + 2 * (LAST - line)))
    x_ahead = jnp.minimum(PAIRS, ahead + 1)
    loop(jnp.where(line >= 12, 1, 0), jnp.where(helped, 1, x_ahead), spread_x)
    swap_copy(0).wait_recv()
    swap_copy(1).wait_recv()
    loop(0, ahead, forward)
    for n in (2, 3, 4):
        swap_copy(n).wait_recv()

    @pl.when(line < LAST)
    def _():
        info_copy(0).wait_recv()

    def step(n):
        @pl.when(line < LAST)
        def _():
            home(n)
            pass_on(n)

        k = n // 2

        @pl.when(top & (lax.rem(n, 2) == 0) & (k + x_ahead < PAIRS))
        def _():
            spread_x(k + x_ahead)

        @pl.when((lax.rem(n, 2) == 1) & (k + ahead < PAIRS))
        def _():
            forward(k + ahead)

        @pl.when((line == 0) & (n > 0))
        def _():
            finish(n - 1)

        backward(n)

    loop(0, MB, step)

    @pl.when(line == 0)
    def _():
        finish(MB - 1)

    for n in range(5):
        swap_copy(n).wait_send()

    @pl.when(helped)
    def _():
        info_copy(2).wait_send()
        drain(send_x.at[0, pl.ds(0, EXPERTS - 1)], x_send)
        drain(x_ref.at[pl.ds(2 * TOK, (PAIRS - 1) * 2 * TOK)], help_send)

    @pl.when(jnp.logical_not(helped))
    def _():
        drain(send_x.at[:, pl.ds(0, EXPERTS - 1)], x_send)

    @pl.when(line > 0)
    def _():
        info_copy(0).wait_send()
        drain(send_r, r_send)
        drain(out_ref, o_recv)

    @pl.when(line == 0)
    def _():
        drain(send_r.at[:, pl.ds(0, EXPERTS - 1)], r_send)

    @pl.when(top)
    def _():
        info_copy(1).wait_send()

    @pl.when(line < LAST)
    def _():
        drain(send_g.at[:, pl.ds(0, EXPERTS - 1)], g_send)
        drain(g_here, o_send)

    @pl.when((line > 0) & (line < LAST))
    def _():
        drain(g_here, p_send)


def chain(x, og, pairs, wg, wu, wd):
    vmem = pl.BlockSpec(memory_space=pltpu.VMEM)
    anywhere = pl.BlockSpec(memory_space=pl.ANY)
    x_blocks = (PAIRS, EXPERTS, 4 * ROWS, LANES)
    blocks = (MB, EXPERTS, 2 * ROWS, LANES)
    rows = (MB, 2, TOK_ROWS, LANES)
    dma = pltpu.SemaphoreType.DMA
    return pl.pallas_call(
        chain_kernel,
        out_shape=jax.ShapeDtypeStruct(rows, BF16),
        in_specs=[vmem] * 3 + [anywhere] * 3,
        out_specs=vmem,
        scratch_shapes=[pltpu.VMEM((2, D, HID), BF16)] * 3
        + [pltpu.VMEM((2, HID, D), BF16)] * 2
        + [pltpu.VMEM((HID, D), BF16)]
        + [pltpu.VMEM((4, MB, LANES), F32)] * 3
        + [pltpu.VMEM((MB * TOK, D), BF16)]
        + [pltpu.VMEM(x_blocks, BF16)]
        + [pltpu.VMEM(blocks, BF16)] * 2
        + [pltpu.VMEM(x_blocks, BF16)]
        + [pltpu.VMEM(blocks, BF16)] * 3
        + [pltpu.VMEM(rows, BF16)] * 2
        + [
            pltpu.VMEM((MB, 2, PAD, 2 * HID), F32),
            pltpu.VMEM((2 * PAD, D), BF16),
            pltpu.VMEM((FOLD * PAD, LANES), BF16),
            pltpu.VMEM((FOLD * PAD, PAIR_ROWS), BF16),
            pltpu.VMEM((PAIR_ROWS, FOLD * PAD), BF16),
        ]
        + [dma((3,)), dma((5,)), dma((5,)), dma((3,)), dma((3,)), dma, dma((PAIRS,))]
        + [dma] * 5
        + [dma((PAIRS,)), dma((MB, 2)), dma((MB, 2)), dma((MB, 2)), dma((MB, 2)), dma]
        + [pltpu.SemaphoreType.REGULAR],
        compiler_params=pltpu.CompilerParams(
            collective_id=0, has_side_effects=True, vmem_limit_bytes=60 * 1024 * 1024
        ),
    )(x, og, pairs, wg, wu, wd)


def on_device(layer_inputs, expert_ids, gates, w_gate, w_up, w_down, out_grad):
    pairs = jnp.concatenate([expert_ids[0].astype(F32), gates[0].astype(F32)], axis=-1)
    pairs = jnp.tile(pairs.transpose(2, 0, 1), (1, 1, FOLD))
    out = chain(
        layer_inputs.reshape(MB * TOK, D), out_grad.reshape(MB * TOK, D), pairs,
        w_gate[0], w_up[0], w_down[0],
    )
    out = out.reshape(MB, 2, FOLD, TOK, LANES).transpose(0, 3, 1, 2, 4).reshape(MB, TOK, D)
    return out[None]


def solution(mesh):
    placed = (
        P("section", None, "expert", None),
        P("section", None, "expert", None),
        P("section", None, "expert", None),
        P("section", None, "expert"),
        P("section", None, "expert"),
        P("section", "expert", None),
        P(None, "expert", None),
    )
    return jax.shard_map(
        on_device,
        mesh=mesh,
        in_specs=placed,
        out_specs=P("section", None, "expert", None),
        check_vma=False,
    )
```

```python
import jax
import jax.numpy as jnp
from jax import lax
from jax.experimental import pallas as pl
from jax.experimental.pallas import tpu as pltpu
from jax.sharding import PartitionSpec as P

EXPERTS = 8
CAP = 3
SLOTS = EXPERTS * CAP
MB = 16
PAIRS = MB // 2
TOK = 8
D = 4096
FOLD = 16
LANES = 128
HALF = FOLD * LANES
ROWS = CAP * FOLD
PAIR_ROWS = SLOTS * FOLD
TOK_ROWS = TOK * FOLD
PAD = 32
HID = 256
LINES = 16
LAST = LINES - 1
FIRST = 3
FAR_FIRST = (4, 3, 5, 2, 6, 1, 7)
MESH = pl.DeviceIdType.MESH
BF16 = jnp.bfloat16
F32 = jnp.float32


def matmul(a, b):
    return lax.dot_general(a, b, (((1,), (0,)), ((), ())), preferred_element_type=F32)


def iota(shape, dim):
    return lax.broadcasted_iota(jnp.int32, shape, dim)


def chain_kernel(
    x_ref, og_ref, pairs_ref, wg_hbm, wu_hbm, wd_hbm,
    out_ref,
    wg, wu, wd, wgt, wut, wd_raw, info, comb_info, top_info, x_help,
    send_x, send_g, send_r, recv_x, recv_g, recv_r, recv_last,
    g_prev, g_here, saved, lhs, folded, unfold_mat, fold_mat, dispatch_mat, combine_mat,
    own_sems, swap_send, swap_recv, info_send, info_recv, help_send, help_recv,
    x_send, g_send, r_send, p_send, o_send,
    x_recv, g_recv, r_recv, last_recv, p_recv, o_recv, turn,
):
    line = lax.axis_index("section")
    i = lax.axis_index("expert")
    z = i // 2
    c = lax.rem(i, 2)

    def off(by):
        return lax.rem(line + by, LINES)

    def at(section, chip):
        return {"section": section, "expert": chip * 2 + c}

    def other(d):
        return lax.rem(z + d, EXPERTS)

    first = line == FIRST
    top = line == LAST
    helped = (line >= 12) & (line < LAST)
    helper = line < 3
    sibling = {"section": line, "expert": z * 2 + 1 - c}
    barrier = pltpu.get_barrier_semaphore()

    def greet(device):
        pl.semaphore_signal(barrier, inc=1, device_id=device, device_id_type=MESH)

    greet(sibling)
    for d in range(1, EXPERTS):
        greet(at(line, other(d)))
    for d in range(EXPERTS):
        greet(at(off(1), other(d)))
        greet(at(off(15), other(d)))

    @pl.when(top)
    def _():
        for d in range(EXPERTS):
            greet(at(FIRST, other(d)))

    @pl.when(first)
    def _():
        for d in range(EXPERTS):
            greet(at(LAST, other(d)))

    @pl.when(helped)
    def _():
        for d in range(EXPERTS):
            greet(at(off(4), other(d)))

    @pl.when(helper)
    def _():
        greet(at(off(12), z))

    raw = ((wg_hbm, wg.at[c]), (wu_hbm, wu.at[c]), (wd_hbm, wd_raw))

    def own_copy(n):
        return pltpu.make_async_copy(raw[n][0], raw[n][1], own_sems.at[n])

    for n in (2, 0, 1):
        own_copy(n).start()

    whole = (wg, wu, wd, wgt, wut)

    def swap_copy(n):
        return pltpu.make_async_remote_copy(
            src_ref=whole[n].at[c], dst_ref=whole[n].at[c], send_sem=swap_send.at[n],
            recv_sem=swap_recv.at[n], device_id=sibling, device_id_type=MESH,
        )

    ids = (pairs_ref[0], pairs_ref[1])
    token = iota((MB, LANES), 1) & 7
    slots = [jnp.zeros((MB, LANES), F32), jnp.zeros((MB, LANES), F32)]
    for r in range(1, TOK):
        for k in range(2):
            earlier = pltpu.roll(ids[k], r, 1)
            for q in range(2):
                slots[q] += jnp.where((earlier == ids[q]) & (token >= r), 1.0, 0.0)
    for q in range(2):
        info[q] = ids[q] * CAP + slots[q]
        info[2 + q] = pairs_ref[2 + q]

    r0, r1 = iota((FOLD * PAD, PAIR_ROWS), 0), iota((FOLD * PAD, PAIR_ROWS), 1)
    hit = ((r0 & 31) == (r1 >> 4)) & ((r0 >> 5) == (r1 & 15))
    unfold_mat[...] = jnp.where(hit, 1.0, 0.0).astype(BF16)
    r0, r1 = iota((PAIR_ROWS, FOLD * PAD), 0), iota((PAIR_ROWS, FOLD * PAD), 1)
    hit = ((r1 & 31) == (r0 >> 4)) & ((r1 >> 5) == (r0 & 15))
    fold_mat[...] = jnp.where(hit, 1.0, 0.0).astype(BF16)

    extra = jnp.where(top | first | helper, EXPERTS, jnp.where(helped, 1, 0))
    pl.semaphore_wait(barrier, 3 * EXPERTS + extra)

    def info_copy(n):
        return pltpu.make_async_remote_copy(
            src_ref=info, dst_ref=(comb_info, top_info, top_info)[n], send_sem=info_send.at[n],
            recv_sem=info_recv.at[n], device_id=at((off(15), FIRST, off(4))[n], z), device_id_type=MESH,
        )

    @pl.when(line > 0)
    def _():
        info_copy(0).start()

    @pl.when(top)
    def _():
        info_copy(1).start()

    @pl.when(helped)
    def _():
        info_copy(2).start()

    def matrix(ref, m, first, second):
        place = (iota((PAIR_ROWS, TOK_ROWS), 0) >> 4).astype(F32)
        same = (iota((PAIR_ROWS, TOK_ROWS), 0) & 15) == (iota((PAIR_ROWS, TOK_ROWS), 1) >> 3)
        row = pl.ds(m, 1)
        value = jnp.where(ref[0, row] == place, first, jnp.where(ref[1, row] == place, second, 0.0))
        return jnp.where(same, value, 0.0)

    def dispatch_matrix(ref, m):
        return matrix(ref, m, 1.0, 1.0).astype(BF16)

    def combine_matrix(ref, m):
        row = pl.ds(m, 1)
        return matrix(ref, m, ref[2, row], ref[3, row]).T.astype(BF16)

    def half(h):
        return pl.ds(h * ROWS, ROWS)

    def part(value):
        return value.astype(BF16).reshape(EXPERTS, ROWS, LANES)

    def fold_pair(ref, p):
        both = ref[pl.ds(pl.multiple_of(p * 2 * TOK, 2 * TOK), 2 * TOK), :].astype(F32)
        result = []
        for b in range(2):
            rows = both[b * TOK : (b + 1) * TOK]
            halves = []
            for h in range(2):
                columns = [rows[:, h * HALF + j * LANES : h * HALF + (j + 1) * LANES] for j in range(FOLD)]
                halves.append(jnp.concatenate(columns, axis=0).astype(BF16))
            result.append(halves)
        return result

    def fill_x(ref, p, from_info):
        values = fold_pair(ref, p)
        for b in range(2):
            dispatch = dispatch_matrix(from_info, p * 2 + b)
            for h in range(2):
                send_x[p, :, pl.ds((b * 2 + h) * ROWS, ROWS), :] = part(matmul(dispatch, values[b][h]))

    def x_copy(p, to, to_line):
        return pltpu.make_async_remote_copy(
            src_ref=send_x.at[p, to], dst_ref=recv_x.at[p, z], send_sem=x_send,
            recv_sem=x_recv.at[p], device_id=at(to_line, to), device_id_type=MESH,
        )

    def pair_rows(p):
        return pl.ds(pl.multiple_of(p * 2 * TOK, 2 * TOK), 2 * TOK)

    def help_copy(p):
        return pltpu.make_async_remote_copy(
            src_ref=x_ref.at[pair_rows(p)], dst_ref=x_help.at[pair_rows(p)], send_sem=help_send,
            recv_sem=help_recv.at[p], device_id=at(off(4), z), device_id_type=MESH,
        )

    def spread_x(p):
        fill_x(x_ref, p, info)
        for d in FAR_FIRST:
            x_copy(p, other(d), line).start()
        pltpu.make_async_copy(send_x.at[p, z], recv_x.at[p, z], x_recv.at[p]).start()

    def g_copy(m, h, to, to_line):
        return pltpu.make_async_remote_copy(
            src_ref=send_g.at[m, to, half(h)], dst_ref=recv_g.at[m, z, half(h)], send_sem=g_send,
            recv_sem=g_recv.at[m, h], device_id=at(to_line, to), device_id_type=MESH,
        )

    def spread_g(m, h, dispatch, rows):
        send_g[m, :, half(h), :] = part(matmul(dispatch, rows))
        for d in FAR_FIRST:
            g_copy(m, h, other(d), line).start()
        pltpu.make_async_copy(
            send_g.at[m, z, half(h)], recv_g.at[m, z, half(h)], g_recv.at[m, h]
        ).start()

    def spread_top(m, h, dispatch, rows):
        send_g[m, :, half(h), :] = part(matmul(dispatch, rows))
        for d in FAR_FIRST + (0,):
            g_copy(m, h, other(d), LAST).start()

    def arrived(ref, m, h, sem):
        block = ref.at[m, :, half(h)]
        pltpu.make_async_copy(block, block, sem.at[m, h]).wait()

    def drain(ref, sem):
        pltpu.make_async_copy(ref, ref, sem).wait()

    def unfold(rows, b, h):
        rows = matmul(unfold_mat[...], rows.reshape(PAIR_ROWS, LANES)).astype(BF16)
        for j in range(FOLD):
            columns = slice(h * HALF + j * LANES, h * HALF + (j + 1) * LANES)
            lhs[b * PAD : (b + 1) * PAD, columns] = rows[j * PAD : (j + 1) * PAD]

    def forward(p):
        drain(recv_x.at[p], x_recv.at[p])
        for b in range(2):
            for h in range(2):
                unfold(recv_x[p, :, pl.ds((b * 2 + h) * ROWS, ROWS), :], b, h)
        for k in range(2):
            hidden = slice(k * HID, (k + 1) * HID)
            gate = matmul(lhs[...], wg[k])
            value = matmul(lhs[...], wu[k])
            sig = jax.nn.sigmoid(gate)
            act = gate * sig
            coef = value * (sig * (1.0 + gate * (1.0 - sig)))
            for b in range(2):
                saved[p * 2 + b, 0, :, hidden] = act[b * PAD : (b + 1) * PAD]
                saved[p * 2 + b, 1, :, hidden] = coef[b * PAD : (b + 1) * PAD]

    def send_back(m, h):
        @pl.when(line > 0)
        def _():
            for d in FAR_FIRST + (0,):
                to = other(d)
                pltpu.make_async_remote_copy(
                    src_ref=send_r.at[m, to, half(h)], dst_ref=recv_r.at[m, z, half(h)], send_sem=r_send,
                    recv_sem=r_recv.at[m, h], device_id=at(off(15), to), device_id_type=MESH,
                ).start()

        @pl.when(line == 0)
        def _():
            for d in FAR_FIRST:
                to = other(d)
                pltpu.make_async_remote_copy(
                    src_ref=send_r.at[m, to, half(h)], dst_ref=recv_last.at[m, z, half(h)], send_sem=r_send,
                    recv_sem=last_recv.at[m, h], device_id=at(line, to), device_id_type=MESH,
                ).start()
            pltpu.make_async_copy(
                send_r.at[m, z, half(h)], recv_last.at[m, z, half(h)], last_recv.at[m, h]
            ).start()

    def backward(m):
        sums = [None, None]
        for h in range(2):
            arrived(recv_g, m, h, g_recv)
            if h == 0:
                @pl.when((line < LAST) & (c == 0))
                def _():
                    pl.semaphore_signal(turn, inc=1, device_id=sibling, device_id_type=MESH)

            unfold(recv_g[m, :, half(h), :], 0, h)
            columns = slice(h * HALF, (h + 1) * HALF)
            for k in range(2):
                term = matmul(lhs[:PAD, columns], wd[k, columns, :])
                sums[k] = term if h == 0 else sums[k] + term
        pieces = []
        for k in range(2):
            hidden = slice(k * HID, (k + 1) * HID)
            pieces.append(
                ((sums[k] * saved[m, 1, :, hidden]).astype(BF16), (sums[k] * saved[m, 0, :, hidden]).astype(BF16))
            )
        width = 4 * LANES
        for h in range(2):
            for n in range(HALF // width):
                columns = slice(h * HALF + n * width, h * HALF + (n + 1) * width)
                total = matmul(pieces[0][0], wgt[0, :, columns])
                total += matmul(pieces[0][1], wut[0, :, columns])
                total += matmul(pieces[1][0], wgt[1, :, columns])
                total += matmul(pieces[1][1], wut[1, :, columns])
                rows = total.astype(BF16)
                for q in range(4):
                    j = n * 4 + q
                    folded[j * PAD : (j + 1) * PAD, :] = rows[:, q * LANES : (q + 1) * LANES]
            send_r[m, :, half(h), :] = part(matmul(fold_mat[...], folded[...]))
            send_back(m, h)

    def home(m):
        @pl.when(c == 1)
        def _():
            pl.semaphore_wait(turn, 1)

        for h in range(2):
            @pl.when(line < LAST - 1)
            def _():
                drain(g_prev.at[m, h], p_recv.at[m, h])

            arrived(recv_r, m, h, r_recv)
            mixed = matmul(combine_mat[...], recv_r[m, :, half(h), :].reshape(PAIR_ROWS, LANES))
            rows = (g_prev[m, h].astype(F32) + mixed).astype(BF16)
            g_here[m, h] = rows
            spread_g(m, h, dispatch_mat[...], rows)

    def prepare(m):
        dispatch_mat[...] = dispatch_matrix(info, m)
        combine_mat[...] = combine_matrix(comb_info, m)

    def pass_on(m):
        @pl.when(line > 0)
        def _():
            for h in range(2):
                pltpu.make_async_remote_copy(
                    src_ref=g_here.at[m, h], dst_ref=g_prev.at[m, h], send_sem=p_send,
                    recv_sem=p_recv.at[m, h], device_id=at(off(15), z), device_id_type=MESH,
                ).start()

        pltpu.make_async_remote_copy(
            src_ref=g_here.at[m], dst_ref=out_ref.at[m], send_sem=o_send, recv_sem=o_recv,
            device_id=at(off(1), z), device_id_type=MESH,
        ).start()

    def finish(m):
        combine = combine_matrix(info, m)
        for h in range(2):
            arrived(recv_last, m, h, last_recv)
            mixed = matmul(combine, recv_last[m, :, half(h), :].reshape(PAIR_ROWS, LANES))
            out_ref[m, h] = (g_here[m, h].astype(F32) + mixed).astype(BF16)

    def loop(low, high, body):
        def run(n, carry):
            body(n)
            return carry

        lax.fori_loop(low, high, run, 0)

    @pl.when(line >= 12)
    def _():
        spread_x(0)

    @pl.when(helped)
    def _():
        loop(1, PAIRS, lambda p: help_copy(p).start())

    own_copy(0).wait()
    swap_copy(0).start()
    own_copy(1).wait()
    swap_copy(1).start()

    @pl.when(first)
    def _():
        info_copy(1).wait_recv()

        def start(p):
            values = fold_pair(og_ref, p)
            for b in range(2):
                dispatch = dispatch_matrix(top_info, p * 2 + b)
                for h in range(2):
                    spread_top(p * 2 + b, h, dispatch, values[b][h])

        loop(0, PAIRS, start)

    own_copy(2).wait()

    def turn_down(n):
        columns = pl.ds(pl.multiple_of(n * HID, HID), HID)
        wd[c, columns, :] = wd_raw[:, columns].T

    loop(0, D // HID, turn_down)
    swap_copy(2).start()

    def turn_up(n):
        rows = pl.ds(pl.multiple_of(n * HID, HID), HID)
        wgt[c, :, rows] = wg[c, rows, :].T
        wut[c, :, rows] = wu[c, rows, :].T

    loop(0, D // HID, turn_up)
    swap_copy(3).start()
    swap_copy(4).start()

    @pl.when(helper)
    def _():
        info_copy(2).wait_recv()

        def start(p):
            drain(x_help.at[pair_rows(p)], help_recv.at[p])
            fill_x(x_help, p, top_info)
            for d in FAR_FIRST + (0,):
                x_copy(p, other(d), off(12)).start()
            drain(send_x.at[p], x_send)

        loop(1, PAIRS, start)

    @pl.when(line == LAST - 1)
    def _():
        def start(p):
            values = fold_pair(og_ref, p)
            for b in range(2):
                for h in range(2):
                    g_prev[p * 2 + b, h] = values[b][h]

        loop(0, PAIRS, start)

    @pl.when(first)
    def _():
        drain(send_g, g_send)

    ahead = jnp.where(helped, 1 + LAST - line, jnp.minimum(PAIRS, 1 + 2 * (LAST - line)))
    x_ahead = jnp.minimum(PAIRS, ahead + 1)
    loop(jnp.where(line >= 12, 1, 0), jnp.where(helped, 1, x_ahead), spread_x)
    swap_copy(0).wait_recv()
    swap_copy(1).wait_recv()
    loop(0, ahead, forward)
    for n in (2, 3, 4):
        swap_copy(n).wait_recv()

    @pl.when(line < LAST)
    def _():
        info_copy(0).wait_recv()
        prepare(0)

    def step(n):
        @pl.when(line < LAST)
        def _():
            home(n)
            pass_on(n)
            prepare(jnp.minimum(n + 1, MB - 1))

        k = n // 2

        @pl.when(top & (lax.rem(n, 2) == 0) & (k + x_ahead < PAIRS))
        def _():
            spread_x(k + x_ahead)

        @pl.when((lax.rem(n, 2) == 1) & (k + ahead < PAIRS))
        def _():
            forward(k + ahead)

        @pl.when((line == 0) & (n > 0))
        def _():
            finish(n - 1)

        backward(n)

    loop(0, MB, step)

    @pl.when(line == 0)
    def _():
        finish(MB - 1)

    for n in range(5):
        swap_copy(n).wait_send()

    @pl.when(helped)
    def _():
        info_copy(2).wait_send()
        drain(send_x.at[0, pl.ds(0, EXPERTS - 1)], x_send)
        drain(x_ref.at[pl.ds(2 * TOK, (PAIRS - 1) * 2 * TOK)], help_send)

    @pl.when(jnp.logical_not(helped))
    def _():
        drain(send_x.at[:, pl.ds(0, EXPERTS - 1)], x_send)

    @pl.when(line > 0)
    def _():
        info_copy(0).wait_send()
        drain(send_r, r_send)
        drain(out_ref, o_recv)

    @pl.when(line == 0)
    def _():
        drain(send_r.at[:, pl.ds(0, EXPERTS - 1)], r_send)

    @pl.when(top)
    def _():
        info_copy(1).wait_send()

    @pl.when(line < LAST)
    def _():
        drain(send_g.at[:, pl.ds(0, EXPERTS - 1)], g_send)
        drain(g_here, o_send)

    @pl.when((line > 0) & (line < LAST))
    def _():
        drain(g_here, p_send)


def chain(x, og, pairs, wg, wu, wd):
    vmem = pl.BlockSpec(memory_space=pltpu.VMEM)
    anywhere = pl.BlockSpec(memory_space=pl.ANY)
    x_blocks = (PAIRS, EXPERTS, 4 * ROWS, LANES)
    blocks = (MB, EXPERTS, 2 * ROWS, LANES)
    rows = (MB, 2, TOK_ROWS, LANES)
    dma = pltpu.SemaphoreType.DMA
    return pl.pallas_call(
        chain_kernel,
        out_shape=jax.ShapeDtypeStruct(rows, BF16),
        in_specs=[vmem] * 3 + [anywhere] * 3,
        out_specs=vmem,
        scratch_shapes=[pltpu.VMEM((2, D, HID), BF16)] * 3
        + [pltpu.VMEM((2, HID, D), BF16)] * 2
        + [pltpu.VMEM((HID, D), BF16)]
        + [pltpu.VMEM((4, MB, LANES), F32)] * 3
        + [pltpu.VMEM((MB * TOK, D), BF16)]
        + [pltpu.VMEM(x_blocks, BF16)]
        + [pltpu.VMEM(blocks, BF16)] * 2
        + [pltpu.VMEM(x_blocks, BF16)]
        + [pltpu.VMEM(blocks, BF16)] * 3
        + [pltpu.VMEM(rows, BF16)] * 2
        + [
            pltpu.VMEM((MB, 2, PAD, 2 * HID), F32),
            pltpu.VMEM((2 * PAD, D), BF16),
            pltpu.VMEM((FOLD * PAD, LANES), BF16),
            pltpu.VMEM((FOLD * PAD, PAIR_ROWS), BF16),
            pltpu.VMEM((PAIR_ROWS, FOLD * PAD), BF16),
            pltpu.VMEM((PAIR_ROWS, TOK_ROWS), BF16),
            pltpu.VMEM((TOK_ROWS, PAIR_ROWS), BF16),
        ]
        + [dma((3,)), dma((5,)), dma((5,)), dma((3,)), dma((3,)), dma, dma((PAIRS,))]
        + [dma] * 5
        + [dma((PAIRS,)), dma((MB, 2)), dma((MB, 2)), dma((MB, 2)), dma((MB, 2)), dma]
        + [pltpu.SemaphoreType.REGULAR],
        compiler_params=pltpu.CompilerParams(
            collective_id=0, has_side_effects=True, vmem_limit_bytes=60 * 1024 * 1024
        ),
    )(x, og, pairs, wg, wu, wd)


def on_device(layer_inputs, expert_ids, gates, w_gate, w_up, w_down, out_grad):
    pairs = jnp.concatenate([expert_ids[0].astype(F32), gates[0].astype(F32)], axis=-1)
    pairs = jnp.tile(pairs.transpose(2, 0, 1), (1, 1, FOLD))
    out = chain(
        layer_inputs.reshape(MB * TOK, D), out_grad.reshape(MB * TOK, D), pairs,
        w_gate[0], w_up[0], w_down[0],
    )
    out = out.reshape(MB, 2, FOLD, TOK, LANES).transpose(0, 3, 1, 2, 4).reshape(MB, TOK, D)
    return out[None]


def solution(mesh):
    placed = (
        P("section", None, "expert", None),
        P("section", None, "expert", None),
        P("section", None, "expert", None),
        P("section", None, "expert"),
        P("section", None, "expert"),
        P("section", "expert", None),
        P(None, "expert", None),
    )
    return jax.shard_map(
        on_device,
        mesh=mesh,
        in_specs=placed,
        out_specs=P("section", None, "expert", None),
        check_vma=False,
    )
```
